512 devices in a mesh: ov: 64 (over z, y_hi, core), vec: 8 (over x, y_lo).
Axes of the slice: x: 4, y: 4 (y_hi: 2, y_lo: 2; y = y_hi * 2 + y_lo), z: 16, core: 2. Of those that a mesh axis runs over, the one named last changes fastest.
Arguments:
- chol_vectors: bfloat16 [196608, 4096], P('ov', 'vec'), may hold values from -6 to 6
- amplitudes: bfloat16 [196608, 256], P('ov'), may hold values from -0.013671875 to 0.013671875
- sigma_prior: bfloat16 [196608, 256], P(('ov', 'vec')), may hold values from -4 to 4
Outputs:
- sigma_cycle: bfloat16 [196608, 256], P(('ov', 'vec'))
The draws below stay inside these ranges and needn't reach their ends.
All inputs are finite; a program needn't handle non-finite values.
Results may differ from the reference program's by a relative error of at most 0.0065.
Values may be sent and summed in bfloat16 or wider, within the bound.
No kernel may reach another device: no remote copies, remote signals or barrier semaphores. Data moves between devices by JAX's collectives and lax.ppermute only.
A program may use at most 64 MiB of HBM per device.

```python
import jax
import jax.numpy as jnp
from jax import lax

OV = 196608
NV = 4096
JB = 256


def with_spikes(values, key, source, target, parts, factor):
    def block_of(dim):
        return (jnp.arange(values.shape[dim]) // (values.shape[dim] // parts)).reshape((-1,) + (1,) * (values.ndim - 1 - dim))

    one_side = jax.random.permutation(key, parts)[block_of(target)]
    second = (block_of(target) + parts // 2) % parts
    return jnp.where((block_of(source) == one_side) | (block_of(source) == second), factor * values, values)


def steps_of(key, dims, cuts, low, high):
    gain, own = 1.0, jax.random.fold_in(key, 6)
    for axis_at, blocks in cuts:
        draws = jnp.exp(jax.random.uniform(jax.random.fold_in(own, axis_at), (blocks,), jnp.float32, low / len(cuts), high / len(cuts)))
        gain = gain * jnp.repeat(draws, dims[axis_at] // blocks).reshape([-1 if axis == axis_at else 1 for axis in range(len(dims))])
    return gain


def bell_draw(own_key, shape, deviation, bound, pieces=(), held_as=jnp.bfloat16):
    gain = steps_of(own_key, shape, pieces, -0.22, 0.18) if pieces else 1.0
    result = jax.random.normal(own_key, shape, jnp.float32) * deviation * gain
    return jnp.minimum(jnp.maximum(result, -bound), bound).astype(held_as)


def gaussian_with(rng, extent, width, reach, cuts, heavy, dtype=jnp.bfloat16):
    values = width * jax.random.normal(rng, extent, jnp.float32)
    if cuts:
        values = values * steps_of(rng, extent, cuts, -0.22, 0.18)
    return jnp.clip(with_spikes(values, jax.random.fold_in(rng, 3), *heavy), -reach, reach).astype(dtype)


def setup_inputs(seed: int = 0) -> dict:
    splits = jax.random.split(jax.random.key(seed), 4)
    chol_vectors = gaussian_with(splits[0], (OV, NV), 0.177, 6.0, ((0, 64), (1, 8)), (1, 0, 64, 4.0))
    amplitudes = bell_draw(splits[1], (OV, JB), OV ** -0.5, 0.013671875, ((0, 64),))
    sigma_prior = bell_draw(splits[2], (OV, JB), 0.5, 4.0, ((0, 512),))
    return {"chol_vectors": chol_vectors, "amplitudes": amplitudes, "sigma_prior": sigma_prior}


def reference(chol_vectors, amplitudes, sigma_prior):
    contract = (((0,), (0,)), ((), ()))
    coupling = lax.dot_general(chol_vectors, amplitudes, contract, preferred_element_type=jnp.float32)
    coupling_bf = coupling.astype(jnp.bfloat16)
    cycle = jnp.dot(chol_vectors, coupling_bf, preferred_element_type=jnp.float32)
    return (sigma_prior.astype(jnp.float32) + cycle).astype(jnp.bfloat16)
```

```python
import jax
import jax.numpy as jnp
from jax import lax
from jax.experimental import pallas as pl
from jax.experimental.pallas import tpu as pltpu
from jax.sharding import Mesh
from jax.sharding import PartitionSpec as P

FAR, NEAR, YH, CORE, VEC = "z_far", "z_near", "y_hi", "core", "vec"
OV = (FAR, NEAR, YH, CORE)
BLOCK = (NEAR, YH)


def exchange(blocks, axes):
    return lax.all_to_all(blocks, axes, split_axis=0, concat_axis=0, tiled=True)


def sum_of_blocks(blocks):
    return blocks.astype(jnp.float32).sum(axis=0).astype(jnp.bfloat16)


def scatter_sum(x, axes):
    return sum_of_blocks(exchange(x.reshape(lax.axis_size(axes), -1, x.shape[-1]), axes))


def copies(x, axes):
    return exchange(jnp.broadcast_to(x, (lax.axis_size(axes), *x.shape)), axes)


def gather(x, axes):
    return copies(x, axes).reshape(-1, x.shape[-1])


def product_kernel(l_ref, c_ref, out_ref):
    out_ref[...] = jnp.dot(
        l_ref[...], c_ref[...], preferred_element_type=jnp.float32
    ).astype(jnp.bfloat16)


def product(chol, coupling):
    rows, depth = chol.shape
    cols = coupling.shape[1]
    tile = rows // 4
    return pl.pallas_call(
        product_kernel,
        grid=(4,),
        in_specs=[
            pl.BlockSpec((tile, depth), lambda i: (i, 0)),
            pl.BlockSpec((depth, cols), lambda i: (0, 0)),
        ],
        out_specs=pl.BlockSpec((tile, cols), lambda i: (i, 0)),
        out_shape=jax.ShapeDtypeStruct((rows, cols), jnp.bfloat16),
        cost_estimate=pl.CostEstimate(
            flops=2 * rows * depth * cols,
            bytes_accessed=2 * (rows * depth + depth * cols + rows * cols),
            transcendentals=0,
        ),
    )(chol, coupling)


def body(chol_vectors, amplitudes, sigma_prior):
    contract = (((0,), (0,)), ((), ()))
    partial = lax.dot_general(
        chol_vectors, amplitudes, contract, preferred_element_type=jnp.float32
    ).astype(jnp.bfloat16)
    piece = scatter_sum(scatter_sum(partial, CORE), BLOCK)
    piece = sum_of_blocks(copies(piece, FAR))
    coupling = gather(gather(piece, BLOCK), CORE)
    share = product(chol_vectors, coupling)
    arrived = exchange(share.reshape(lax.axis_size(VEC), -1, share.shape[-1]), VEC)
    cycle = arrived.astype(jnp.float32).sum(axis=0)
    return (sigma_prior.astype(jnp.float32) + cycle).astype(jnp.bfloat16)


def solution(mesh):
    finer = Mesh(mesh.devices.reshape(4, 4, 2, 2, mesh.shape["vec"]), (*OV, VEC))
    placed = (P(OV, VEC), P(OV, None), P((*OV, VEC), None))
    return jax.shard_map(
        body, mesh=finer, in_specs=placed, out_specs=P((*OV, VEC), None), check_vma=False
    )
```

```python
import jax
import jax.numpy as jnp
from jax import lax
from jax.experimental import pallas as pl
from jax.experimental.pallas import tpu as pltpu
from jax.sharding import Mesh
from jax.sharding import PartitionSpec as P

FAR, NEAR, YH, CORE, X, YL = "z_far", "z_near", "y_hi", "core", "x", "y_lo"
SIZES = (4, 4, 2, 2, 4, 2)
OV, VEC = (FAR, NEAR, YH, CORE), (X, YL)
SWAP = [(0, 1), (1, 0)]
LIMIT = 24 << 20
WHOLE = pl.BlockSpec(memory_space=pltpu.VMEM)
IN_HBM = pl.BlockSpec(memory_space=pltpu.HBM)
ROWS_BY_ROWS = (((0,), (0,)), ((), ()))
COLUMNS_BY_COLUMNS = (((1,), (1,)), ((), ()))


def in_hbm(x):
    return pltpu.with_memory_space_constraint(x, pltpu.HBM)


def in_vmem(x):
    return pltpu.with_memory_space_constraint(x, pltpu.VMEM)


def exchange(blocks, axes):
    return lax.all_to_all(blocks, axes, split_axis=0, concat_axis=0, tiled=True)


def copies(x, axes):
    return exchange(jnp.broadcast_to(x, (lax.axis_size(axes), *x.shape)), axes)


def summed(blocks):
    return blocks.astype(jnp.float32).sum(axis=0).astype(jnp.bfloat16)


def coupling_kernel(l_hbm, a_hbm, part_ref, kept_ref, sent_hbm, l_ref, a_ref, total_ref, l_sems, a_sems, sent_sems):
    mine = lax.axis_index(YL)
    blocks = l_sems.shape[0] // 2
    size = kept_ref.shape[0] // blocks

    def source(slot, block):
        start = (2 * block + (mine + slot) % 2) * size
        return pl.ds(pl.multiple_of(start, size), size)

    def fetches(k):
        slot, block = 1 - k // blocks, k % blocks
        rows = pl.ds(block * size, size)
        held = l_ref if slot else kept_ref
        return (
            pltpu.make_async_copy(a_hbm.at[source(slot, block)], a_ref.at[slot, rows], a_sems.at[k]),
            pltpu.make_async_copy(l_hbm.at[source(slot, block)], held.at[rows], l_sems.at[k]),
        )

    def passing(block):
        rows = pl.ds(block * size, size)
        return pltpu.make_async_copy(l_ref.at[rows], sent_hbm.at[rows], sent_sems.at[block])

    for k in range(2 * blocks):
        for copy in fetches(k):
            copy.start()
    for k in range(0, 2 * blocks, 2):
        for copy in (*fetches(k), *fetches(k + 1)):
            copy.wait()
        slot, rows = 1 - k // blocks, pl.ds(k % blocks * size, 2 * size)
        if slot:
            passing(k).start()
            passing(k + 1).start()
        held = l_ref if slot else kept_ref
        term = lax.dot_general(
            a_ref[slot, rows], held[rows], ROWS_BY_ROWS, preferred_element_type=jnp.float32
        )
        if k == 0:
            total_ref[...] = term
        elif k < 2 * blocks - 2:
            total_ref[...] += term
        else:
            part_ref[...] = (total_ref[...] + term).astype(jnp.bfloat16)
    for block in range(blocks):
        passing(block).wait()


def coupling_part(chol, amplitudes):
    rows, depth = chol.shape
    cols = amplitudes.shape[1]
    blocks = lax.axis_size(X)
    half = jax.ShapeDtypeStruct((rows // 2, depth), jnp.bfloat16)
    return pl.pallas_call(
        coupling_kernel,
        in_specs=[IN_HBM] * 2,
        out_specs=[WHOLE, WHOLE, IN_HBM],
        out_shape=[jax.ShapeDtypeStruct((cols, depth), jnp.bfloat16), half, pltpu.HBM(half.shape, half.dtype)],
        scratch_shapes=[
            pltpu.VMEM(half.shape, half.dtype),
            pltpu.VMEM((2, rows // 2, cols), jnp.bfloat16),
            pltpu.VMEM((cols, depth), jnp.float32),
            pltpu.SemaphoreType.DMA((2 * blocks,)),
            pltpu.SemaphoreType.DMA((2 * blocks,)),
            pltpu.SemaphoreType.DMA((blocks,)),
        ],
        compiler_params=pltpu.CompilerParams(vmem_limit_bytes=LIMIT),
        cost_estimate=pl.CostEstimate(
            flops=2 * rows * depth * cols,
            bytes_accessed=2 * (2 * rows * depth + rows * cols + depth * cols),
            transcendentals=0,
        ),
    )(in_hbm(chol), in_hbm(amplitudes))


def product_kernel(kept_ref, came_ref, own_ref, other_ref, out_ref, c_ref):
    mine, core = lax.axis_index(YL), lax.axis_index(CORE)
    blocks, size, _ = out_ref.shape
    half = own_ref.shape[1]
    for at, ref in ((core, own_ref), (1 - core, other_ref)):
        c_ref[:, pl.ds(pl.multiple_of(at * half, half), half), :] = ref[...]
    own, other = c_ref[mine], c_ref[1 - mine]

    def by(x, coupling):
        return lax.dot_general(x, coupling, COLUMNS_BY_COLUMNS, preferred_element_type=jnp.float32)

    for k in range(blocks):
        rows = pl.ds(k * size, size)
        out_ref[k] = (by(kept_ref[rows], own) + by(came_ref[rows], other)).astype(jnp.bfloat16)


def product(kept, came, own, other):
    rows, depth = kept.shape
    cols = 2 * own.shape[1]
    blocks = lax.axis_size(X)
    return pl.pallas_call(
        product_kernel,
        in_specs=[WHOLE] * 4,
        out_specs=WHOLE,
        out_shape=jax.ShapeDtypeStruct((blocks, rows // blocks, cols), jnp.bfloat16),
        scratch_shapes=[pltpu.VMEM((2, cols, depth), jnp.bfloat16)],
        compiler_params=pltpu.CompilerParams(vmem_limit_bytes=LIMIT),
        cost_estimate=pl.CostEstimate(
            flops=4 * kept.size * cols,
            bytes_accessed=2 * (2 * kept.size + 2 * own.size + rows * cols),
            transcendentals=0,
        ),
    )(kept, in_vmem(came), own, other)


def finish_kernel(arrived_ref, prior_ref, out_ref):
    cycle = arrived_ref[0].astype(jnp.float32)
    for k in range(1, arrived_ref.shape[0]):
        cycle += arrived_ref[k].astype(jnp.float32)
    out_ref[...] = (prior_ref[...].astype(jnp.float32) + cycle).astype(jnp.bfloat16)


def finish(arrived, prior):
    return pl.pallas_call(
        finish_kernel,
        in_specs=[WHOLE, WHOLE],
        out_specs=WHOLE,
        out_shape=jax.ShapeDtypeStruct(prior.shape, jnp.bfloat16),
        compiler_params=pltpu.CompilerParams(vmem_limit_bytes=LIMIT),
        cost_estimate=pl.CostEstimate(
            flops=arrived.size, bytes_accessed=2 * (arrived.size + 2 * prior.size), transcendentals=0
        ),
    )(arrived, prior)


def body(chol_vectors, amplitudes, sigma_prior):
    part, kept, sent = coupling_part(chol_vectors, amplitudes)
    came = lax.ppermute(sent, YL, SWAP)
    near = (CORE, NEAR, YH)
    piece = summed(exchange(part.reshape(lax.axis_size(near), -1, part.shape[-1]), near))
    piece = summed(copies(piece, FAR))
    half = copies(piece, (YL, NEAR, YH))
    half = half.reshape(2, -1, half.shape[-1])
    share = product(kept, came, half, lax.ppermute(half, CORE, SWAP))
    return finish(exchange(share, X), sigma_prior)


def solution(mesh):
    finer = Mesh(mesh.devices.reshape(SIZES), (*OV, *VEC))
    placed = (P(OV, VEC), P(OV, None), P((*OV, *VEC), None))
    return jax.shard_map(
        body, mesh=finer, in_specs=placed, out_specs=P((*OV, *VEC), None), check_vma=False
    )
```

```python
import jax
import jax.numpy as jnp
from jax import lax
from jax.experimental import pallas as pl
from jax.experimental.pallas import tpu as pltpu
from jax.sharding import Mesh
from jax.sharding import PartitionSpec as P

FAR, NEAR, YH, CORE, X, YL = "z_far", "z_near", "y_hi", "core", "x", "y_lo"
SIZES = (4, 4, 2, 2, 4, 2)
OV, VEC = (FAR, NEAR, YH, CORE), (X, YL)
SWAP = [(0, 1), (1, 0)]
PAIRS = ([(0, 1), (1, 0), (2, 3), (3, 2)], [(1, 2), (2, 1), (3, 0), (0, 3)])
LIMIT = 24 << 20
WHOLE = pl.BlockSpec(memory_space=pltpu.VMEM)
IN_HBM = pl.BlockSpec(memory_space=pltpu.HBM)
ROWS_BY_ROWS = (((0,), (0,)), ((), ()))
COLUMNS_BY_COLUMNS = (((1,), (1,)), ((), ()))


def in_hbm(x):
    return pltpu.with_memory_space_constraint(x, pltpu.HBM)


def in_vmem(x):
    return pltpu.with_memory_space_constraint(x, pltpu.VMEM)


def exchange(blocks, axes):
    return lax.all_to_all(blocks, axes, split_axis=0, concat_axis=0, tiled=True)


def copies(x, axes):
    return exchange(jnp.broadcast_to(x, (lax.axis_size(axes), *x.shape)), axes)


def summed(blocks):
    return blocks.astype(jnp.float32).sum(axis=0)


def coupling_kernel(l_hbm, a_hbm, part_ref, kept_ref, sent_hbm, l_ref, a_ref, total_ref, l_sems, a_sems, sent_sems):
    mine = lax.axis_index(YL)
    blocks = l_sems.shape[0] // 2
    size = kept_ref.shape[0] // blocks

    def source(slot, block):
        start = (2 * block + (mine + slot) % 2) * size
        return pl.ds(pl.multiple_of(start, size), size)

    def fetches(k):
        slot, block = 1 - k // blocks, k % blocks
        rows = pl.ds(block * size, size)
        held = l_ref if slot else kept_ref
        return (
            pltpu.make_async_copy(a_hbm.at[source(slot, block)], a_ref.at[slot, rows], a_sems.at[k]),
            pltpu.make_async_copy(l_hbm.at[source(slot, block)], held.at[rows], l_sems.at[k]),
        )

    def passing(block):
        rows = pl.ds(block * size, size)
        return pltpu.make_async_copy(l_ref.at[rows], sent_hbm.at[rows], sent_sems.at[block])

    for k in range(2 * blocks):
        for copy in fetches(k):
            copy.start()
    for k in range(0, 2 * blocks, 2):
        for copy in (*fetches(k), *fetches(k + 1)):
            copy.wait()
        slot, rows = 1 - k // blocks, pl.ds(k % blocks * size, 2 * size)
        if slot:
            passing(k).start()
            passing(k + 1).start()
        held = l_ref if slot else kept_ref
        term = lax.dot_general(
            a_ref[slot, rows], held[rows], ROWS_BY_ROWS, preferred_element_type=jnp.float32
        )
        if k == 0:
            total_ref[...] = term
        elif k < 2 * blocks - 2:
            total_ref[...] += term
        else:
            part_ref[...] = (total_ref[...] + term).astype(jnp.bfloat16)
    for block in range(blocks):
        passing(block).wait()


def coupling_part(chol, amplitudes):
    rows, depth = chol.shape
    cols = amplitudes.shape[1]
    blocks = lax.axis_size(X)
    half = jax.ShapeDtypeStruct((rows // 2, depth), jnp.bfloat16)
    return pl.pallas_call(
        coupling_kernel,
        in_specs=[IN_HBM] * 2,
        out_specs=[WHOLE, WHOLE, IN_HBM],
        out_shape=[jax.ShapeDtypeStruct((cols, depth), jnp.bfloat16), half, pltpu.HBM(half.shape, half.dtype)],
        scratch_shapes=[
            pltpu.VMEM(half.shape, half.dtype),
            pltpu.VMEM((2, rows // 2, cols), jnp.bfloat16),
            pltpu.VMEM((cols, depth), jnp.float32),
            pltpu.SemaphoreType.DMA((2 * blocks,)),
            pltpu.SemaphoreType.DMA((2 * blocks,)),
            pltpu.SemaphoreType.DMA((blocks,)),
        ],
        compiler_params=pltpu.CompilerParams(vmem_limit_bytes=LIMIT),
        cost_estimate=pl.CostEstimate(
            flops=2 * rows * depth * cols,
            bytes_accessed=2 * (2 * rows * depth + rows * cols + depth * cols),
            transcendentals=0,
        ),
    )(in_hbm(chol), in_hbm(amplitudes))


def product_kernel(kept_ref, came_ref, own_ref, other_ref, out_ref, c_ref):
    mine, core = lax.axis_index(YL), lax.axis_index(CORE)
    blocks, size, _ = out_ref.shape
    half = own_ref.shape[1]
    for at, ref in ((core, own_ref), (1 - core, other_ref)):
        c_ref[:, pl.ds(pl.multiple_of(at * half, half), half), :] = ref[...]
    own, other = c_ref[mine], c_ref[1 - mine]

    def by(x, coupling):
        return lax.dot_general(x, coupling, COLUMNS_BY_COLUMNS, preferred_element_type=jnp.float32)

    for k in range(blocks):
        rows = pl.ds(k * size, size)
        out_ref[k] = (by(kept_ref[rows], own) + by(came_ref[rows], other)).astype(jnp.bfloat16)


def product(kept, came, own, other):
    rows, depth = kept.shape
    cols = 2 * own.shape[1]
    blocks = lax.axis_size(X)
    return pl.pallas_call(
        product_kernel,
        in_specs=[WHOLE] * 4,
        out_specs=WHOLE,
        out_shape=jax.ShapeDtypeStruct((blocks, rows // blocks, cols), jnp.bfloat16),
        scratch_shapes=[pltpu.VMEM((2, cols, depth), jnp.bfloat16)],
        compiler_params=pltpu.CompilerParams(vmem_limit_bytes=LIMIT),
        cost_estimate=pl.CostEstimate(
            flops=4 * kept.size * cols,
            bytes_accessed=2 * (2 * kept.size + 2 * own.size + rows * cols),
            transcendentals=0,
        ),
    )(kept, in_vmem(came), own, other)


def finish_kernel(arrived_ref, prior_ref, out_ref):
    cycle = arrived_ref[0].astype(jnp.float32)
    for k in range(1, arrived_ref.shape[0]):
        cycle += arrived_ref[k].astype(jnp.float32)
    out_ref[...] = (prior_ref[...].astype(jnp.float32) + cycle).astype(jnp.bfloat16)


def finish(arrived, prior):
    return pl.pallas_call(
        finish_kernel,
        in_specs=[WHOLE, WHOLE],
        out_specs=WHOLE,
        out_shape=jax.ShapeDtypeStruct(prior.shape, jnp.bfloat16),
        compiler_params=pltpu.CompilerParams(vmem_limit_bytes=LIMIT),
        cost_estimate=pl.CostEstimate(
            flops=arrived.size, bytes_accessed=2 * (arrived.size + 2 * prior.size), transcendentals=0
        ),
    )(arrived, prior)


def body(chol_vectors, amplitudes, sigma_prior):
    part, kept, sent = coupling_part(chol_vectors, amplitudes)
    came = lax.ppermute(sent, YL, SWAP)
    near = (CORE, NEAR, YH)
    piece = summed(exchange(part.reshape(lax.axis_size(near), -1, part.shape[-1]), near))
    for pairs in PAIRS:
        piece += lax.ppermute(piece, FAR, pairs)
    piece = piece.astype(jnp.bfloat16)
    half = copies(piece, (YL, NEAR, YH))
    half = half.reshape(2, -1, half.shape[-1])
    share = product(kept, came, half, lax.ppermute(half, CORE, SWAP))
    return finish(exchange(share, X), sigma_prior)


def solution(mesh):
    finer = Mesh(mesh.devices.reshape(SIZES), (*OV, *VEC))
    placed = (P(OV, VEC), P(OV, None), P((*OV, *VEC), None))
    return jax.shard_map(
        body, mesh=finer, in_specs=placed, out_specs=P((*OV, *VEC), None), check_vma=False
    )
```

```python
import jax
import jax.numpy as jnp
from jax import lax
from jax.experimental import pallas as pl
from jax.experimental.pallas import tpu as pltpu
from jax.sharding import Mesh
from jax.sharding import PartitionSpec as P

FAR, NEAR, YH, CORE, YL = "z_far", "z_near", "y_hi", "core", "y_lo"
X = ("x_hi", "x_lo")
SIZES = (4, 4, 2, 2, 2, 2, 2)
OV, VEC = (FAR, NEAR, YH, CORE), (*X, YL)
SWAP = [(0, 1), (1, 0)]
PAIRS = ([(0, 1), (1, 0), (2, 3), (3, 2)], [(1, 2), (2, 1), (3, 0), (0, 3)])
LIMIT = 24 << 20
WHOLE = pl.BlockSpec(memory_space=pltpu.VMEM)
IN_HBM = pl.BlockSpec(memory_space=pltpu.HBM)
ROWS_BY_ROWS = (((0,), (0,)), ((), ()))
COLUMNS_BY_COLUMNS = (((1,), (1,)), ((), ()))


def in_hbm(x):
    return pltpu.with_memory_space_constraint(x, pltpu.HBM)


def in_vmem(x):
    return pltpu.with_memory_space_constraint(x, pltpu.VMEM)


def exchange(blocks, axes):
    return lax.all_to_all(blocks, axes, split_axis=0, concat_axis=0, tiled=True)


def copies(x, axes):
    return exchange(jnp.broadcast_to(x, (lax.axis_size(axes), *x.shape)), axes)


def summed(blocks):
    return blocks.astype(jnp.float32).sum(axis=0)


def coupling_kernel(l_hbm, a_hbm, part_ref, kept_ref, sent_hbm, l_ref, a_ref, total_ref, l_sems, a_sems, sent_sems):
    mine = lax.axis_index(YL)
    blocks = l_sems.shape[0] // 2
    size = kept_ref.shape[0] // blocks

    def source(slot, block):
        start = (2 * block + (mine + slot) % 2) * size
        return pl.ds(pl.multiple_of(start, size), size)

    def fetches(k):
        slot, block = 1 - k // blocks, k % blocks
        rows = pl.ds(block * size, size)
        held = l_ref if slot else kept_ref
        return (
            pltpu.make_async_copy(a_hbm.at[source(slot, block)], a_ref.at[slot, rows], a_sems.at[k]),
            pltpu.make_async_copy(l_hbm.at[source(slot, block)], held.at[rows], l_sems.at[k]),
        )

    def passing(block):
        rows = pl.ds(block * size, size)
        return pltpu.make_async_copy(l_ref.at[rows], sent_hbm.at[rows], sent_sems.at[block])

    for k in range(2 * blocks):
        for copy in fetches(k):
            copy.start()
    for k in range(0, 2 * blocks, 2):
        for copy in (*fetches(k), *fetches(k + 1)):
            copy.wait()
        slot, rows = 1 - k // blocks, pl.ds(k % blocks * size, 2 * size)
        if slot:
            passing(k).start()
            passing(k + 1).start()
        held = l_ref if slot else kept_ref
        term = lax.dot_general(
            a_ref[slot, rows], held[rows], ROWS_BY_ROWS, preferred_element_type=jnp.float32
        )
        if k == 0:
            total_ref[...] = term
        elif k < 2 * blocks - 2:
            total_ref[...] += term
        else:
            part_ref[...] = (total_ref[...] + term).astype(jnp.bfloat16)
    for block in range(blocks):
        passing(block).wait()


def coupling_part(chol, amplitudes):
    rows, depth = chol.shape
    cols = amplitudes.shape[1]
    blocks = lax.axis_size(X)
    half = jax.ShapeDtypeStruct((rows // 2, depth), jnp.bfloat16)
    return pl.pallas_call(
        coupling_kernel,
        in_specs=[IN_HBM] * 2,
        out_specs=[WHOLE, WHOLE, IN_HBM],
        out_shape=[jax.ShapeDtypeStruct((cols, depth), jnp.bfloat16), half, pltpu.HBM(half.shape, half.dtype)],
        scratch_shapes=[
            pltpu.VMEM(half.shape, half.dtype),
            pltpu.VMEM((2, rows // 2, cols), jnp.bfloat16),
            pltpu.VMEM((cols, depth), jnp.float32),
            pltpu.SemaphoreType.DMA((2 * blocks,)),
            pltpu.SemaphoreType.DMA((2 * blocks,)),
            pltpu.SemaphoreType.DMA((blocks,)),
        ],
        compiler_params=pltpu.CompilerParams(vmem_limit_bytes=LIMIT),
        cost_estimate=pl.CostEstimate(
            flops=2 * rows * depth * cols,
            bytes_accessed=2 * (2 * rows * depth + rows * cols + depth * cols),
            transcendentals=0,
        ),
    )(in_hbm(chol), in_hbm(amplitudes))


def product_kernel(kept_ref, came_ref, own_ref, other_ref, out_ref, c_ref):
    mine, core = lax.axis_index(YL), lax.axis_index(CORE)
    blocks, size, _ = out_ref.shape
    parts, _, part, _ = own_ref.shape
    for at, ref in ((core, own_ref), (1 - core, other_ref)):
        for k in range(parts):
            c_ref[:, pl.ds(pl.multiple_of((at * parts + k) * part, part), part), :] = ref[k]
    own, other = c_ref[mine], c_ref[1 - mine]

    def by(x, coupling):
        return lax.dot_general(x, coupling, COLUMNS_BY_COLUMNS, preferred_element_type=jnp.float32)

    for k in range(blocks):
        rows = pl.ds(k * size, size)
        out_ref[2 * (k % 2) + k // 2] = (by(kept_ref[rows], own) + by(came_ref[rows], other)).astype(jnp.bfloat16)


def product(kept, came, own, other):
    rows, depth = kept.shape
    cols = 2 * own.shape[0] * own.shape[2]
    blocks = lax.axis_size(X)
    return pl.pallas_call(
        product_kernel,
        in_specs=[WHOLE] * 4,
        out_specs=WHOLE,
        out_shape=jax.ShapeDtypeStruct((blocks, rows // blocks, cols), jnp.bfloat16),
        scratch_shapes=[pltpu.VMEM((own.shape[1], cols, depth), jnp.bfloat16)],
        compiler_params=pltpu.CompilerParams(vmem_limit_bytes=LIMIT),
        cost_estimate=pl.CostEstimate(
            flops=4 * kept.size * cols,
            bytes_accessed=2 * (2 * kept.size + 2 * own.size + rows * cols),
            transcendentals=0,
        ),
    )(kept, in_vmem(came), own, other)


def finish_kernel(arrived_ref, prior_ref, out_ref):
    cycle = arrived_ref[0].astype(jnp.float32)
    for k in range(1, arrived_ref.shape[0]):
        cycle += arrived_ref[k].astype(jnp.float32)
    out_ref[...] = (prior_ref[...].astype(jnp.float32) + cycle).astype(jnp.bfloat16)


def finish(arrived, prior):
    return pl.pallas_call(
        finish_kernel,
        in_specs=[WHOLE, WHOLE],
        out_specs=WHOLE,
        out_shape=jax.ShapeDtypeStruct(prior.shape, jnp.bfloat16),
        compiler_params=pltpu.CompilerParams(vmem_limit_bytes=LIMIT),
        cost_estimate=pl.CostEstimate(
            flops=arrived.size, bytes_accessed=2 * (arrived.size + 2 * prior.size), transcendentals=0
        ),
    )(arrived, prior)


def body(chol_vectors, amplitudes, sigma_prior):
    part, kept, sent = coupling_part(chol_vectors, amplitudes)
    came = lax.ppermute(sent, YL, SWAP)
    near = (CORE, YH, NEAR)
    piece = summed(exchange(part.reshape(lax.axis_size(near), -1, part.shape[-1]), near))
    for pairs in PAIRS:
        piece += lax.ppermute(piece, FAR, pairs)
    piece = piece.astype(jnp.bfloat16)
    half = copies(piece, (YH, YL, NEAR))
    half = half.reshape(lax.axis_size(YH), lax.axis_size(YL), -1, half.shape[-1])
    share = product(kept, came, half, lax.ppermute(half, CORE, SWAP))
    return finish(exchange(share, X[::-1]), sigma_prior)


def solution(mesh):
    finer = Mesh(mesh.devices.reshape(SIZES), (*OV, *VEC))
    placed = (P(OV, VEC), P(OV, None), P((*OV, *VEC), None))
    return jax.shard_map(
        body, mesh=finer, in_specs=placed, out_specs=P((*OV, *VEC), None), check_vma=False
    )
```

```python
import jax
import jax.numpy as jnp
from jax import lax
from jax.experimental import pallas as pl
from jax.experimental.pallas import tpu as pltpu
from jax.sharding import Mesh
from jax.sharding import PartitionSpec as P

FAR, NEAR, YH, CORE, X, YL = "z_far", "z_near", "y_hi", "core", "x", "y_lo"
SIZES = (4, 4, 2, 2, 4, 2)
OV, VEC = (FAR, NEAR, YH, CORE), (X, YL)
SWAP = [(0, 1), (1, 0)]
RING = ([(0, 1), (1, 0), (2, 3), (3, 2)], [(1, 2), (2, 1), (3, 0), (0, 3)])
PAIRS = [
    [(2 * i + core, 2 * j + core) for core in (0, 1) for i, j in RING[step ^ (1 - core)]] for step in (0, 1)
]
LIMIT = 24 << 20
WHOLE = pl.BlockSpec(memory_space=pltpu.VMEM)
IN_HBM = pl.BlockSpec(memory_space=pltpu.HBM)
ROWS_BY_ROWS = (((0,), (0,)), ((), ()))
COLUMNS_BY_COLUMNS = (((1,), (1,)), ((), ()))


def in_hbm(x):
    return pltpu.with_memory_space_constraint(x, pltpu.HBM)


def in_vmem(x):
    return pltpu.with_memory_space_constraint(x, pltpu.VMEM)


def exchange(blocks, axes):
    return lax.all_to_all(blocks, axes, split_axis=0, concat_axis=0, tiled=True)


def copies(x, axes):
    return exchange(jnp.broadcast_to(x, (lax.axis_size(axes), *x.shape)), axes)


def summed(blocks):
    return blocks.astype(jnp.float32).sum(axis=0)


def coupling_kernel(l_hbm, a_hbm, part_ref, kept_ref, sent_hbm, l_ref, a_ref, total_ref, l_sems, a_sems, sent_sems):
    mine = lax.axis_index(YL)
    blocks = l_sems.shape[0] // 2
    size = kept_ref.shape[0] // blocks

    def source(slot, block):
        start = (2 * block + (mine + slot) % 2) * size
        return pl.ds(pl.multiple_of(start, size), size)

    def fetches(k):
        slot, block = 1 - k // blocks, k % blocks
        rows = pl.ds(block * size, size)
        held = l_ref if slot else kept_ref
        return (
            pltpu.make_async_copy(a_hbm.at[source(slot, block)], a_ref.at[slot, rows], a_sems.at[k]),
            pltpu.make_async_copy(l_hbm.at[source(slot, block)], held.at[rows], l_sems.at[k]),
        )

    def passing(block):
        rows = pl.ds(block * size, size)
        return pltpu.make_async_copy(l_ref.at[rows], sent_hbm.at[rows], sent_sems.at[block])

    for k in range(2 * blocks):
        for copy in fetches(k):
            copy.start()
    for k in range(0, 2 * blocks, 2):
        for copy in (*fetches(k), *fetches(k + 1)):
            copy.wait()
        slot, rows = 1 - k // blocks, pl.ds(k % blocks * size, 2 * size)
        if slot:
            passing(k).start()
            passing(k + 1).start()
        held = l_ref if slot else kept_ref
        term = lax.dot_general(
            a_ref[slot, rows], held[rows], ROWS_BY_ROWS, preferred_element_type=jnp.float32
        )
        if k == 0:
            total_ref[...] = term
        elif k < 2 * blocks - 2:
            total_ref[...] += term
        else:
            part_ref[...] = (total_ref[...] + term).astype(jnp.bfloat16)
    for block in range(blocks):
        passing(block).wait()


def coupling_part(chol, amplitudes):
    rows, depth = chol.shape
    cols = amplitudes.shape[1]
    blocks = lax.axis_size(X)
    half = jax.ShapeDtypeStruct((rows // 2, depth), jnp.bfloat16)
    return pl.pallas_call(
        coupling_kernel,
        in_specs=[IN_HBM] * 2,
        out_specs=[WHOLE, WHOLE, IN_HBM],
        out_shape=[jax.ShapeDtypeStruct((cols, depth), jnp.bfloat16), half, pltpu.HBM(half.shape, half.dtype)],
        scratch_shapes=[
            pltpu.VMEM(half.shape, half.dtype),
            pltpu.VMEM((2, rows // 2, cols), jnp.bfloat16),
            pltpu.VMEM((cols, depth), jnp.float32),
            pltpu.SemaphoreType.DMA((2 * blocks,)),
            pltpu.SemaphoreType.DMA((2 * blocks,)),
            pltpu.SemaphoreType.DMA((blocks,)),
        ],
        compiler_params=pltpu.CompilerParams(vmem_limit_bytes=LIMIT),
        cost_estimate=pl.CostEstimate(
            flops=2 * rows * depth * cols,
            bytes_accessed=2 * (2 * rows * depth + rows * cols + depth * cols),
            transcendentals=0,
        ),
    )(in_hbm(chol), in_hbm(amplitudes))


def product_kernel(kept_ref, came_ref, own_ref, other_ref, out_ref, c_ref):
    mine, core = lax.axis_index(YL), lax.axis_index(CORE)
    blocks, size, _ = out_ref.shape
    half = own_ref.shape[1]
    for at, ref in ((core, own_ref), (1 - core, other_ref)):
        c_ref[:, pl.ds(pl.multiple_of(at * half, half), half), :] = ref[...]
    own, other = c_ref[mine], c_ref[1 - mine]

    def by(x, coupling):
        return lax.dot_general(x, coupling, COLUMNS_BY_COLUMNS, preferred_element_type=jnp.float32)

    for k in range(blocks):
        rows = pl.ds(k * size, size)
        out_ref[k] = (by(kept_ref[rows], own) + by(came_ref[rows], other)).astype(jnp.bfloat16)


def product(kept, came, own, other):
    rows, depth = kept.shape
    cols = 2 * own.shape[1]
    blocks = lax.axis_size(X)
    return pl.pallas_call(
        product_kernel,
        in_specs=[WHOLE] * 4,
        out_specs=WHOLE,
        out_shape=jax.ShapeDtypeStruct((blocks, rows // blocks, cols), jnp.bfloat16),
        scratch_shapes=[pltpu.VMEM((2, cols, depth), jnp.bfloat16)],
        compiler_params=pltpu.CompilerParams(vmem_limit_bytes=LIMIT),
        cost_estimate=pl.CostEstimate(
            flops=4 * kept.size * cols,
            bytes_accessed=2 * (2 * kept.size + 2 * own.size + rows * cols),
            transcendentals=0,
        ),
    )(kept, in_vmem(came), own, other)


def finish_kernel(arrived_ref, prior_ref, out_ref):
    cycle = arrived_ref[0].astype(jnp.float32)
    for k in range(1, arrived_ref.shape[0]):
        cycle += arrived_ref[k].astype(jnp.float32)
    out_ref[...] = (prior_ref[...].astype(jnp.float32) + cycle).astype(jnp.bfloat16)


def finish(arrived, prior):
    return pl.pallas_call(
        finish_kernel,
        in_specs=[WHOLE, WHOLE],
        out_specs=WHOLE,
        out_shape=jax.ShapeDtypeStruct(prior.shape, jnp.bfloat16),
        compiler_params=pltpu.CompilerParams(vmem_limit_bytes=LIMIT),
        cost_estimate=pl.CostEstimate(
            flops=arrived.size, bytes_accessed=2 * (arrived.size + 2 * prior.size), transcendentals=0
        ),
    )(arrived, prior)


def body(chol_vectors, amplitudes, sigma_prior):
    part, kept, sent = coupling_part(chol_vectors, amplitudes)
    came = lax.ppermute(sent, YL, SWAP)
    near = (CORE, NEAR, YH)
    piece = summed(exchange(part.reshape(lax.axis_size(near), -1, part.shape[-1]), near))
    for pairs in PAIRS:
        piece += lax.ppermute(piece, (FAR, CORE), pairs)
    piece = piece.astype(jnp.bfloat16)
    half = copies(piece, (YL, NEAR, YH))
    half = half.reshape(2, -1, half.shape[-1])
    share = product(kept, came, half, lax.ppermute(half, CORE, SWAP))
    return finish(exchange(share, X), sigma_prior)


def solution(mesh):
    finer = Mesh(mesh.devices.reshape(SIZES), (*OV, *VEC))
    placed = (P(OV, VEC), P(OV, None), P((*OV, *VEC), None))
    return jax.shard_map(
        body, mesh=finer, in_specs=placed, out_specs=P((*OV, *VEC), None), check_vma=False
    )
```
